256 devices in a mesh: pipe: 4 (over y_lo, core), expert: 64 (over z, y_hi, x).
Axes of the slice: x: 4, y: 4 (y_hi: 2, y_lo: 2; y = y_hi * 2 + y_lo), z: 8, core: 2. Of those that a mesh axis runs over, the one named last changes fastest.
Arguments:
- east_prev: bfloat16 [4, 4096, 7168], P('pipe', 'expert'), may hold values from -6 to 6
- west_prev: bfloat16 [4, 4096, 7168], P('pipe', 'expert'), may hold values from -6 to 6
- east_routes: int32 [4, 4096, 8], P('pipe', 'expert'), may hold values from 0 to 255, all different within a row; in each aligned block of 64 rows (0 to 63, 64 to 127, ..., all dimensions but the last counted through in order) at most 4 rows name the same one
- west_routes: int32 [4, 4096, 8], P('pipe', 'expert'), may hold values from 0 to 255, all different within a row; in each aligned block of 64 rows (0 to 63, 64 to 127, ..., all dimensions but the last counted through in order) at most 4 rows name the same one
- east_affinity: float32 [4, 4096, 8], P('pipe', 'expert'), may hold values from 0.05 to 1
- west_affinity: float32 [4, 4096, 8], P('pipe', 'expert'), may hold values from 0.05 to 1
- norm_gain: float32 [4, 7168], P('pipe'), may hold values from 0.25 to 1.75
- w_gate: bfloat16 [4, 7168, 8192], P('pipe', None, 'expert'), may hold values from -0.0625 to 0.0625
- w_up: bfloat16 [4, 7168, 8192], P('pipe', None, 'expert'), may hold values from -0.0625 to 0.0625
- w_down: bfloat16 [4, 8192, 7168], P('pipe', 'expert'), may hold values from -0.1875 to 0.1875
- scales: int32 [4, 8, 56], P('pipe'), may hold values from -1 to 1
Outputs:
- east_out: bfloat16 [4, 4096, 7168], P('pipe', 'expert')
- west_out: bfloat16 [4, 4096, 7168], P('pipe', 'expert')
The draws below stay inside these ranges and needn't reach their ends.
Inputs may be any that keep to these rules, and one draw needn't show every extreme that they name: `east_routes`: the 8 experts of a token differ. Among the 64 rows of one device, no expert is named more than 4 times, a bound that some block reaches. `west_routes`: the 8 experts of a token differ. Among the 64 rows of one device, no expert is named more than 4 times, a bound that some block reaches.
All inputs are finite; a program needn't handle non-finite values.
Results may differ from the reference program's by a relative error of at most 0.0071.
Values may be sent and summed in bfloat16 or wider, within the bound.
A program may use at most 128 MiB of HBM per device.

```python
import math
import jax
import jax.numpy as jnp
import numpy as np
from jax import lax

D = 7168
ALL_EXP = 256
TOP = 8
FF = 1024
SPLIT = 8
TOK_DEV = 64
CAP = 4
WIN_EXP = 8
TOKENS = 4096
SEGMENTS = 4
N_EXPERT = 64


def set_ends(result, rng, smallest, top_value):
    place = [jax.random.randint(jax.random.fold_in(rng, axis), (), 0, length) for axis, length in enumerate(result.shape)]
    longest = result.shape.index(max(result.shape))
    neighbour = place[:longest] + [(place[longest] + 1) % result.shape[longest]] + place[longest + 1:]
    return result.at[tuple(place)].set(smallest).at[tuple(neighbour)].set(top_value)


def block_levels(own_key, dims, cuts, smallest, top_value):
    def one(axis_at, blocks):
        steps = jax.random.uniform(jax.random.fold_in(jax.random.fold_in(own_key, 6), axis_at), (blocks,), jnp.float32, smallest / len(cuts), top_value / len(cuts))
        return jnp.repeat(jnp.exp(steps), dims[axis_at] // blocks).reshape((-1,) + (1,) * (len(dims) - axis_at - 1))

    factor_of = one(*cuts[0])
    for cut in cuts[1:]:
        factor_of = factor_of * one(*cut)
    return factor_of


def shared_out(own_key, own, number, rows, number_of, top, most, slope):
    order = jax.random.permutation(own_key, number_of)
    heavy_load, usual = load_shares(number_of, rows * top, most, slope, True), load_shares(number_of, rows * top, most, slope, False)
    places = jnp.arange(number_of)

    def named(sizes, rotation):
        used = int((sizes > 0).sum())
        fixed = max(1, used // 4)
        shifted = fixed + (places - fixed + rotation * (used - fixed)) % max(1, number_of - fixed)
        return jnp.zeros((number_of,), jnp.int32).at[order[jnp.where(places < fixed, places, shifted)]].set(jnp.asarray(sizes, jnp.int32))

    sizes = jnp.where(number % 4 == 0, named(heavy_load, number // 4), named(usual, number - number // 4 - 1))
    mixed = jax.random.permutation(jax.random.fold_in(own, 3), number_of)
    source_of, sink = mixed[0:number_of // 2 * 2:2], mixed[1:number_of // 2 * 2:2]
    slack = jnp.minimum(sizes[source_of] - 1, most - sizes[sink]) // 2
    slack = jnp.where((source_of == order[0]) | (sink == order[0]) | (sizes[sink] == 0), 0, jnp.maximum(slack, 0))
    shifted = jax.random.randint(jax.random.fold_in(own, 4), (number_of // 2,), 0, 1 << 20) % (slack + 1)
    sizes = sizes.at[source_of].add(-shifted).at[sink].add(shifted)
    items = jnp.searchsorted(jnp.cumsum(sizes), jnp.arange(rows * top), side="right").astype(jnp.int32)
    listing = items.reshape(top, rows).T
    listing = listing[jax.random.permutation(jax.random.fold_in(own, 1), rows)]
    rotation = jax.random.randint(jax.random.fold_in(own, 2), (rows, 1), 0, top)
    return jnp.take_along_axis(listing, (jnp.arange(top)[None, :] + rotation) % top, axis=1)


def load_shares(number_of, total, reach, lean, full):
    weights = [(1 << 20) // math.isqrt(rank ** lean) + 1 for rank in range(1, number_of + 1)]
    largest = reach if full else min(reach, max(-(-total // number_of), total * weights[0] // sum(weights)))
    least = 1 if total - largest >= number_of - 1 else 0
    counts, rest = [largest] + [least] * (number_of - 1), total - largest - least * (number_of - 1)
    while rest > 0:
        candidates = [i for i in range(1, number_of) if counts[i] < largest] or [i for i in range(1, number_of) if counts[i] < reach]
        whole, remaining = sum([weights[i] for i in candidates]), rest
        for i in candidates:
            extra = min(reach - counts[i], max(1, remaining * weights[i] // whole), rest)
            counts[i] = counts[i] + extra
            rest = rest - extra
    return np.array(counts)


def bell_draw(rng, dims, deviation, limit, cuts=(), kind=jnp.bfloat16):
    result = deviation * jax.random.normal(rng, dims, jnp.float32)
    if cuts:
        result = result * block_levels(rng, dims, cuts, -0.22, 0.18)
    return jnp.clip(result, -limit, limit).astype(kind)


def setup_inputs(seed: int = 0) -> dict:
    seeds = jax.random.split(jax.random.key(seed), 12)
    east_prev = bell_draw(seeds[0], (SEGMENTS, TOKENS, D), 1.0, 6.0, ((0, 4), (1, 64)))
    west_prev = bell_draw(seeds[1], (SEGMENTS, TOKENS, D), 1.0, 6.0, ((0, 4), (1, 64)))
    east_routes_keys = jax.random.split(jax.random.fold_in(seeds[2], 1), SEGMENTS * TOKENS // TOK_DEV)
    east_routes_turns = jax.random.permutation(jax.random.fold_in(seeds[2], 3), SEGMENTS * TOKENS // TOK_DEV)
    east_routes = jax.vmap(lambda own, number: shared_out(jax.random.fold_in(seeds[2], 2), own, number, TOK_DEV, ALL_EXP, TOP, CAP, 2))(east_routes_keys, east_routes_turns).reshape((SEGMENTS, TOKENS, TOP))
    west_routes_keys = jax.random.split(jax.random.fold_in(seeds[3], 1), SEGMENTS * TOKENS // TOK_DEV)
    west_routes_turns = jax.random.permutation(jax.random.fold_in(seeds[3], 3), SEGMENTS * TOKENS // TOK_DEV)
    west_routes = jax.vmap(lambda own, number: shared_out(jax.random.fold_in(seeds[3], 2), own, number, TOK_DEV, ALL_EXP, TOP, CAP, 2))(west_routes_keys, west_routes_turns).reshape((SEGMENTS, TOKENS, TOP))
    east_affinity = jnp.clip(jnp.exp(math.log(1.0) - 2.9957323 * jax.random.uniform(seeds[4], (SEGMENTS, TOKENS, TOP), jnp.float32) ** block_levels(seeds[4], (SEGMENTS, TOKENS, TOP), ((0, 4), (1, 64)), -0.2, 0.2)), 0.05, 1.0)
    west_affinity = jnp.clip(jnp.exp(math.log(1.0) - 2.9957323 * jax.random.uniform(seeds[5], (SEGMENTS, TOKENS, TOP), jnp.float32) ** block_levels(seeds[5], (SEGMENTS, TOKENS, TOP), ((0, 4), (1, 64)), -0.2, 0.2)), 0.05, 1.0)
    norm_gain = jnp.clip(1.0 + 0.15 * jax.random.normal(seeds[6], (SEGMENTS, D), jnp.float32), 0.25, 1.75)
    w_gate = bell_draw(seeds[7], (SEGMENTS, D, WIN_EXP * FF), D ** -0.5, 0.0625, ((0, 4), (2, 64)))
    w_up = bell_draw(seeds[8], (SEGMENTS, D, WIN_EXP * FF), D ** -0.5, 0.0625, ((0, 4), (2, 64)))
    w_down = bell_draw(seeds[9], (SEGMENTS, WIN_EXP * FF, D), FF ** -0.5, 0.1875, ((0, 4), (1, 64)))
    scales = set_ends(jax.random.randint(seeds[10], (SEGMENTS, WIN_EXP, D // 128), -1, 2), jax.random.fold_in(seeds[10], 1), -1, 1).astype(jnp.int32)
    return dict(east_prev=east_prev, west_prev=west_prev, east_routes=east_routes, west_routes=west_routes, east_affinity=east_affinity, west_affinity=west_affinity, norm_gain=norm_gain, w_gate=w_gate, w_up=w_up, w_down=w_down, scales=scales)


route_scale = 2.5

def normalize(tokens, gain):
    values = tokens.astype(jnp.float32)
    meansq = lax.optimization_barrier(jnp.mean(values * values, axis=-1, keepdims=True))
    return (values * lax.rsqrt(meansq + 1e-06) * gain).astype(jnp.bfloat16)

def layer_pass(tokens, routes, affinity, gain, w_gate, w_up, w_down, scales):
    normed = normalize(tokens, gain)
    expert_ids = jnp.arange(WIN_EXP, dtype=jnp.int32)
    matches = routes[:, :, None] == expert_ids[None, None, :]
    chosen = lax.optimization_barrier(jnp.sum(matches.astype(jnp.int32), axis=1))
    shares = route_scale * affinity / lax.optimization_barrier(jnp.sum(affinity, axis=1, keepdims=True))
    weights = lax.optimization_barrier(jnp.sum(matches.astype(jnp.float32) * shares[:, :, None], axis=1))
    block_chosen = chosen.reshape(N_EXPERT, TOK_DEV, WIN_EXP)
    block_weights = weights.reshape(N_EXPERT, TOK_DEV, WIN_EXP)
    ranked = (jnp.cumsum(block_chosen, axis=1) - 1).astype(jnp.int32)
    target = jnp.where(block_chosen > 0, ranked, CAP).astype(jnp.int32)
    positions = jnp.broadcast_to(jnp.arange(TOK_DEV, dtype=jnp.int32)[None, :, None], target.shape)
    block_index = jnp.broadcast_to(jnp.arange(N_EXPERT, dtype=jnp.int32)[:, None, None], target.shape)
    expert_index = jnp.broadcast_to(expert_ids[None, None, :], target.shape)
    table = jnp.full((N_EXPERT, WIN_EXP, CAP + 1), TOK_DEV, jnp.int32)
    table = table.at[block_index, expert_index, target].set(positions)
    table = table[:, :, :CAP].reshape(N_EXPERT, WIN_EXP * CAP)
    padded = jnp.concatenate([normed.reshape(N_EXPERT, TOK_DEV, D), jnp.zeros((N_EXPERT, 1, D), jnp.bfloat16)], axis=1)
    slot_rows = jnp.take_along_axis(padded, table[:, :, None], axis=1).reshape(N_EXPERT, WIN_EXP, CAP, D)
    rows_by_expert = jnp.transpose(slot_rows, (1, 0, 2, 3))
    gate_cols = jnp.transpose(w_gate.reshape(D, WIN_EXP, FF), (1, 0, 2))
    up_cols = jnp.transpose(w_up.reshape(D, WIN_EXP, FF), (1, 0, 2))
    down_rows = w_down.reshape(WIN_EXP, FF, D)

    def one_expert(packed):
        expert_rows, gate_part, up_part, down_part, exponents = packed
        factor = jnp.repeat(jnp.exp2(exponents.astype(jnp.float32)), 128).astype(jnp.bfloat16)
        scaled = expert_rows.reshape(N_EXPERT * CAP, D) * factor
        gate_out = jnp.dot(scaled, gate_part, preferred_element_type=jnp.float32)
        up_out = jnp.dot(scaled, up_part, preferred_element_type=jnp.float32)
        hidden = (jax.nn.silu(gate_out) * up_out).astype(jnp.bfloat16)
        pieces = jnp.einsum('rsh,shd->rsd', hidden.reshape(N_EXPERT * CAP, SPLIT, FF // SPLIT).astype(jnp.float32), down_part.reshape(SPLIT, FF // SPLIT, D).astype(jnp.float32))
        rounded = lax.optimization_barrier(pieces.astype(jnp.bfloat16))
        return lax.optimization_barrier(jnp.sum(rounded.astype(jnp.float32), axis=1)).reshape(N_EXPERT, CAP, D)
    expert_out = lax.map(one_expert, (rows_by_expert, gate_cols, up_cols, down_rows, scales))
    clipped = jnp.clip(ranked, 0, CAP - 1).astype(jnp.int32)

    def add_expert(total, packed):
        outputs, ranks, shares_now = packed
        picked = jnp.take_along_axis(outputs, ranks[:, :, None], axis=1)
        return (total + shares_now[:, :, None] * picked, None)
    start = jnp.zeros((N_EXPERT, TOK_DEV, D), jnp.float32)
    total, unused = lax.scan(add_expert, start, (expert_out, jnp.moveaxis(clipped, 2, 0), jnp.moveaxis(block_weights, 2, 0)))
    return total.reshape(TOKENS, D).astype(jnp.bfloat16)

def reference(east_prev, west_prev, east_routes, west_routes, east_affinity, west_affinity, norm_gain, w_gate, w_up, w_down, scales):
    east_in = jnp.roll(east_prev, 1, axis=0)
    west_in = jnp.roll(west_prev, -1, axis=0)
    east_list = []
    west_list = []
    for segment in range(SEGMENTS):
        east_list.append(layer_pass(east_in[segment], east_routes[segment], east_affinity[segment], norm_gain[segment], w_gate[segment], w_up[segment], w_down[segment], scales[segment]))
        west_list.append(layer_pass(west_in[segment], west_routes[segment], west_affinity[segment], norm_gain[segment], w_gate[segment], w_up[segment], w_down[segment], scales[segment]))
    return (jnp.stack(east_list), jnp.stack(west_list))
```

```python
import functools
import jax
import jax.numpy as jnp
from jax import lax
from jax.experimental import pallas as pl
from jax.experimental.pallas import tpu as pltpu
from jax.sharding import PartitionSpec as P

CAP = 4
NX, NY = 4, 2
NJ = NX * NY
NCH = 4
F32, BF16, I32 = jnp.float32, jnp.bfloat16, jnp.int32
MESH = pl.DeviceIdType.MESH
route_scale = 2.5


def cut(total, num, den):
    return (total * num // den) // 128 * 128


def kernel(
    np_, nz, d, tok, nf,
    xe, xw, rte, rtw, afe, afw, gain, wg, wu, wd, scales,
    oute, outw,
    X, RP, RR, AP, W, WD, GS, T1, T2, PK, Q, G, H, O, B, C, F, SP, OUT,
    s_loc, s_out, s_rt, r_rt, s_wd, r_wd, s_a, r_a, s_g, r_g, s_h, r_h, s_b, r_b, s_f, r_f,
):
    oc = d // NJ
    mr = nz * NJ * 2
    blk = 2 * nz
    ca = cut(d, 5, 9)
    qa = max(cut(d, 2, 9), 128)
    p = lax.axis_index("pipe")
    e = lax.axis_index("expert")
    z = e // NJ
    j = e % NJ
    y = j // NX
    x = j % NX
    base = z * NJ
    xr = (x + 1) % NX
    xl = (x + NX - 1) % NX
    x2 = (x + 2) % NX
    yo = 1 - y
    dev_r = (p, base + y * NX + xr)
    dev_l = (p, base + y * NX + xl)
    dev_y = (p, base + yo * NX + x)
    pn = (p + 1) % np_
    pp = (p + np_ - 1) % np_

    def rc(src, dst, ss, rs, dev):
        return pltpu.make_async_remote_copy(
            src_ref=src, dst_ref=dst, send_sem=ss, recv_sem=rs, device_id=dev, device_id_type=MESH
        )

    def drain(ref, sem):
        pltpu.make_async_copy(ref, ref, sem).wait()

    def ocol(o):
        return pl.ds(pl.multiple_of(o * oc, 128), oc)

    local = [
        pltpu.make_async_copy(xe, X.at[0], s_loc.at[0]),
        pltpu.make_async_copy(xw, X.at[1], s_loc.at[1]),
        pltpu.make_async_copy(wg, W.at[:, pl.ds(0, nf)], s_loc.at[2]),
        pltpu.make_async_copy(wu, W.at[:, pl.ds(nf, nf)], s_loc.at[3]),
        pltpu.make_async_copy(
            wd.at[:, ocol(j)], WD.at[pl.ds(pl.multiple_of(j * nf, 128), nf)], s_loc.at[4]
        ),
    ]
    for c in local:
        c.start()

    bar = pltpu.get_barrier_semaphore()

    def greet_z(k, carry):
        zz = (z + k) % nz
        pl.semaphore_signal(bar, inc=1, device_id=(pn, zz * NJ + j), device_id_type=MESH)
        pl.semaphore_signal(bar, inc=1, device_id=(pp, zz * NJ + j), device_id_type=MESH)
        return carry

    lax.fori_loop(0, nz, greet_z, 0)

    def greet_own(k, carry):
        pl.semaphore_signal(
            bar, inc=1, device_id=(p, (z + k) % nz * NJ + j), device_id_type=MESH
        )
        return carry

    lax.fori_loop(1, nz, greet_own, 0)

    def greet_j(k, carry):
        pl.semaphore_signal(bar, inc=1, device_id=(p, base + (j + k) % NJ), device_id_type=MESH)
        return carry

    lax.fori_loop(1, NJ, greet_j, 0)

    RP[...] = jnp.full(RP.shape, -1, I32)
    RP[0, :, 0:tok] = rte[...]
    RP[1, :, 0:tok] = rtw[...]
    AP[...] = jnp.full(AP.shape, 1.0, F32)
    AP[0, :, 0:tok] = afe[...]
    AP[1, :, 0:tok] = afw[...]

    pl.semaphore_wait(bar, 2 * nz + (nz - 1) + (NJ - 1))

    rt_e = rc(RP.at[0], RR.at[0], s_rt.at[0], r_rt.at[0], (pp, e))
    rt_w = rc(RP.at[1], RR.at[1], s_rt.at[1], r_rt.at[1], (pn, e))
    rt_e.start()
    rt_w.start()

    def send_wd(k, carry):
        t = (j + k) % NJ
        rc(
            wd.at[:, ocol(t)],
            WD.at[pl.ds(pl.multiple_of(j * nf, 128), nf)],
            s_wd.at[0],
            r_wd.at[0],
            (p, base + t),
        ).start()
        return carry

    lax.fori_loop(1, NJ, send_wd, 0)

    def iot(shape, dim):
        return lax.broadcasted_iota(I32, shape, dim)

    r_ = iot((mr, mr), 0)
    c_ = iot((mr, mr), 1)
    hit = (
        (r_ // blk == (c_ // 2) % NJ) & ((r_ // 2) % nz == c_ // (2 * NJ)) & (r_ % 2 == c_ % 2)
    )
    T1[...] = hit.astype(F32).astype(BF16)
    hit2 = (
        (c_ // blk == (r_ // 2) % NJ) & ((c_ // 2) % nz == r_ // (2 * NJ)) & (r_ % 2 == c_ % 2)
    )
    T2[...] = hit2.astype(F32).astype(BF16)

    def gain_block(k, carry):
        s = scales[z, k]
        f = jnp.where(s > 0, 2.0, jnp.where(s < 0, 0.5, 1.0)).astype(F32)
        cols = pl.ds(pl.multiple_of(k * 128, 128), 128)
        GS[:, cols] = gain[:, cols] * f
        return carry

    lax.fori_loop(0, d // 128, gain_block, 0)

    lanes = RP.shape[2]
    row = iot((mr, lanes), 0)
    zrow = row // (2 * NJ)
    orow = (row // 2) % NJ
    crow = row % 2
    before = (iot((lanes, lanes), 0) < iot((lanes, lanes), 1)).astype(F32).astype(BF16)

    def slots(rt):
        chosen = jnp.zeros((mr, lanes), F32)
        for k in range(rt.shape[0]):
            chosen = chosen + jnp.where(rt[k : k + 1, :] == zrow, 1.0, 0.0)
        rank = jnp.dot(chosen.astype(BF16), before, preferred_element_type=F32)
        return chosen, rank.astype(I32)

    local[0].wait()
    local[1].wait()
    rt_e.wait_recv()
    rt_w.wait_recv()

    def stage_a(c):
        m, k = c // 2, c % 2
        chosen, rank = slots(RR[m])
        pick = jnp.where((chosen > 0.0) & (rank == 2 * k + crow), 1.0, 0.0)
        acc = jnp.zeros((mr, oc), F32)
        for o in range(NJ):
            part = jnp.where(orow == o, pick, 0.0).astype(BF16)[:, 0:tok]
            acc = acc + jnp.dot(part, X[m, :, o * oc : (o + 1) * oc], preferred_element_type=F32)
        PK[c] = acc.astype(BF16)
        to = (p + 1 + m * (np_ - 2)) % np_

        def send(i, carry):
            t = (z + i) % nz
            rc(
                PK.at[c, pl.ds(pl.multiple_of(t * 2 * NJ, 16), 2 * NJ)],
                Q.at[c, pl.ds(pl.multiple_of(z * 2 * NJ, 16), 2 * NJ)],
                s_a.at[c],
                r_a.at[c],
                (to, t * NJ + j),
            ).start()
            return carry

        lax.fori_loop(0, nz, send, 0)

    def blk_of(c, yy, xx, lo, hi):
        return G.at[c, yy * NX + xx, :, pl.ds(lo, hi - lo)]

    def msg(c, n, yy, xx, lo, hi, dev):
        ref = blk_of(c, yy, xx, lo, hi)
        return rc(ref, ref, s_g.at[c, n], r_g.at[c, n], dev)

    def level0(c):
        return (
            msg(c, 0, y, x, 0, d, dev_r),
            msg(c, 1, y, x, 0, d, dev_l),
            msg(c, 2, y, x, 0, d, dev_y),
        )

    def level1(c):
        return (
            msg(c, 3, y, xl, 0, ca, dev_r),
            msg(c, 4, y, xr, ca, d, dev_l),
            msg(c, 5, y, xl, ca, d, dev_y),
            msg(c, 6, y, xr, ca, d, dev_y),
            msg(c, 7, yo, x, 0, ca, dev_r),
            msg(c, 8, yo, x, 0, ca, dev_l),
        )

    def level2(c):
        return (
            msg(c, 9, y, x2, ca, d, dev_y),
            msg(c, 10, yo, xl, 0, qa, dev_r),
            msg(c, 11, yo, xr, qa, ca, dev_l),
        )

    def stage_b(c):
        drain(Q.at[c], r_a.at[c])
        u = jnp.dot(T1[...], Q[c], preferred_element_type=F32)
        sq = jnp.zeros((blk, 1), F32)
        for o in range(NJ):
            v = u[o * blk : (o + 1) * blk]
            sq = sq + jnp.sum(v * v, axis=1, keepdims=True)
        inv = lax.rsqrt(sq / d + 1e-6)
        for o in range(NJ):
            v = u[o * blk : (o + 1) * blk]
            G[c, j, :, o * oc : (o + 1) * oc] = (v * inv * GS[:, o * oc : (o + 1) * oc]).astype(BF16)
        for s in level0(c):
            s.start()

    def stage_l1(c):
        a, b, w = level0(c)
        m3, m4, m5, m6, m7, m8 = level1(c)
        a.wait_recv()
        m3.start()
        m5.start()
        b.wait_recv()
        m4.start()
        m6.start()
        w.wait_recv()
        m7.start()
        m8.start()

    def stage_l2(c):
        _, m4, _, _, m7, m8 = level1(c)
        m9, m10, m11 = level2(c)
        m4.wait_recv()
        m9.start()
        m7.wait_recv()
        m10.start()
        m8.wait_recv()
        m11.start()

    def stage_d(c):
        m3, _, m5, m6, _, _ = level1(c)
        for s in (m3, m5, m6) + level2(c):
            s.wait_recv()
        kb = d // 7 if d % (7 * 128) == 0 else 128

        def step(i, acc):
            cols = pl.ds(pl.multiple_of(i * kb, 128), kb)
            rows = G[c, :, :, cols].reshape(NJ * blk, kb)
            return acc + jnp.dot(rows, W[cols, :], preferred_element_type=F32)

        acc = lax.fori_loop(0, d // kb, step, jnp.zeros((NJ * blk, 2 * nf), F32))
        gate, up = acc[:, 0:nf], acc[:, nf : 2 * nf]
        H[c, j] = (gate / (1.0 + jnp.exp(-gate)) * up).astype(BF16)

        def send(i, carry):
            t = (j + i) % NJ
            rc(H.at[c, j], H.at[c, j], s_h.at[c], r_h.at[c], (p, base + t)).start()
            return carry

        lax.fori_loop(1, NJ, send, 0)

    def stage_e(c):
        drain(H.at[c, pl.ds(0, NJ - 1)], r_h.at[c])
        hid = jnp.concatenate([H[c, i] for i in range(NJ)], axis=1)
        O[c] = jnp.dot(hid, WD[...], preferred_element_type=F32).astype(BF16)
        own = pl.ds(pl.multiple_of(j * blk, blk), blk)
        B[c, own] = O[c, own]

        def send(i, carry):
            t = (j + i) % NJ
            rc(
                O.at[c, pl.ds(pl.multiple_of(t * blk, blk), blk)],
                B.at[c, own],
                s_b.at[c],
                r_b.at[c],
                (p, base + t),
            ).start()
            return carry

        lax.fori_loop(1, NJ, send, 0)

    def stage_f(c):
        drain(B.at[c, pl.ds(0, (NJ - 1) * blk)], r_b.at[c])
        C[c] = jnp.dot(T2[...], B[c], preferred_element_type=F32).astype(BF16)
        own = pl.ds(pl.multiple_of(z * 2 * NJ, 16), 2 * NJ)
        F[c, own] = C[c, own]

        def send(i, carry):
            t = (z + i) % nz
            rc(
                C.at[c, pl.ds(pl.multiple_of(t * 2 * NJ, 16), 2 * NJ)],
                F.at[c, own],
                s_f.at[c],
                r_f.at[c],
                (p, t * NJ + j),
            ).start()
            return carry

        lax.fori_loop(1, nz, send, 0)

    def spread(m):
        rt = RP[m]
        af = AP[m]
        share = route_scale * af / jnp.sum(af, axis=0, keepdims=True)
        weight = jnp.zeros((mr, lanes), F32)
        for k in range(rt.shape[0]):
            weight = weight + jnp.where(rt[k : k + 1, :] == zrow, share[k : k + 1, :], 0.0)
        chosen, rank = slots(rt)
        olane = (iot((tok, mr), 1) // 2) % NJ
        for k in range(2):
            s = jnp.where((chosen > 0.0) & (rank == 2 * k + crow), weight, 0.0)
            s = jnp.transpose(s)[0:tok]
            hi = s.astype(BF16).astype(F32)
            lo = s - hi
            for h, v in ((0, hi), (1, lo)):
                for o in range(NJ):
                    SP[m, h, o * tok : (o + 1) * tok, k * mr : (k + 1) * mr] = jnp.where(
                        olane == o, v, 0.0
                    ).astype(BF16)

    def stage_g(m):
        for k in range(2):
            drain(F.at[2 * m + k, pl.ds(0, (nz - 1) * 2 * NJ)], r_f.at[2 * m + k])
        rows = F[pl.ds(2 * m, 2)].reshape(2 * mr, oc)
        res = jnp.dot(SP[m, 0], rows, preferred_element_type=F32)
        res = res + jnp.dot(SP[m, 1], rows, preferred_element_type=F32)
        for o in range(NJ):
            OUT[m, :, o * oc : (o + 1) * oc] = res[o * tok : (o + 1) * tok].astype(BF16)

    def pack_loop(c, carry):
        stage_a(c)
        return carry

    lax.fori_loop(0, NCH, pack_loop, 0)
    spread(0)
    spread(1)

    def main(it, carry):
        def when(lag, f):
            c = it - lag
            pl.when((c >= 0) & (c < NCH))(lambda: f(c))

        when(0, stage_b)
        when(1, stage_l1)
        when(2, stage_l2)

        @pl.when(it == 3)
        def _():
            local[2].wait()
            local[3].wait()
            local[4].wait()
            drain(WD.at[pl.ds(0, (NJ - 1) * nf)], r_wd.at[0])

        when(3, stage_d)
        when(4, stage_e)
        when(5, stage_f)

        @pl.when(it == 7)
        def _():
            stage_g(0)
            pltpu.make_async_copy(OUT.at[0], oute, s_out.at[0]).start()

        @pl.when(it == 9)
        def _():
            stage_g(1)
            pltpu.make_async_copy(OUT.at[1], outw, s_out.at[1]).start()

        return carry

    lax.fori_loop(0, 10, main, 0)

    rt_e.wait_send()
    rt_w.wait_send()
    drain(WD.at[pl.ds(0, (NJ - 1) * nf)], s_wd.at[0])

    def finish(c, carry):
        drain(PK.at[c], s_a.at[c])
        for s in level0(c) + level1(c) + level2(c):
            s.wait_send()
        drain(H.at[c, pl.ds(0, NJ - 1)], s_h.at[c])
        drain(O.at[c, pl.ds(0, (NJ - 1) * blk)], s_b.at[c])
        drain(C.at[c, pl.ds(0, (nz - 1) * 2 * NJ)], s_f.at[c])
        return carry

    lax.fori_loop(0, NCH, finish, 0)
    pltpu.make_async_copy(OUT.at[0], oute, s_out.at[0]).wait()
    pltpu.make_async_copy(OUT.at[1], outw, s_out.at[1]).wait()


def body(mesh_shape, xe, xw, rte, rtw, afe, afw, gain, wg, wu, wd, scales):
    np_, ne = mesh_shape
    nz = ne // NJ
    _, tok, d = xe.shape
    nf = wg.shape[2]
    oc = d // NJ
    mr = nz * NJ * 2
    blk = 2 * nz
    top = rte.shape[2]
    any_, vm = pl.BlockSpec(memory_space=pl.ANY), pl.BlockSpec(memory_space=pltpu.VMEM)
    dma = pltpu.SemaphoreType.DMA
    flops = 2 * NCH * NJ * blk * d * 3 * nf
    moved = 2 * 2 * (4 * tok * d + 3 * d * nf)
    outs = pl.pallas_call(
        functools.partial(kernel, np_, nz, d, tok, nf),
        out_shape=[jax.ShapeDtypeStruct((tok, d), BF16)] * 2,
        in_specs=[any_, any_, vm, vm, vm, vm, vm, any_, any_, any_]
        + [pl.BlockSpec(memory_space=pltpu.SMEM)],
        out_specs=[any_, any_],
        scratch_shapes=[
            pltpu.VMEM((2, tok, d), BF16),
            pltpu.VMEM((2, top, 128), I32),
            pltpu.VMEM((2, top, 128), I32),
            pltpu.VMEM((2, top, 128), F32),
            pltpu.VMEM((d, 2 * nf), BF16),
            pltpu.VMEM((NJ * nf, oc), BF16),
            pltpu.VMEM((1, d), F32),
            pltpu.VMEM((mr, mr), BF16),
            pltpu.VMEM((mr, mr), BF16),
            pltpu.VMEM((NCH, mr, oc), BF16),
            pltpu.VMEM((NCH, mr, oc), BF16),
            pltpu.VMEM((NCH, NJ, blk, d), BF16),
            pltpu.VMEM((NCH, NJ, NJ * blk, nf), BF16),
            pltpu.VMEM((NCH, NJ * blk, oc), BF16),
            pltpu.VMEM((NCH, NJ * blk, oc), BF16),
            pltpu.VMEM((NCH, mr, oc), BF16),
            pltpu.VMEM((NCH, mr, oc), BF16),
            pltpu.VMEM((2, 2, NJ * tok, 2 * mr), BF16),
            pltpu.VMEM((2, tok, d), BF16),
            dma((5,)),
            dma((2,)),
            dma((2,)),
            dma((2,)),
            dma((1,)),
            dma((1,)),
            dma((NCH,)),
            dma((NCH,)),
            dma((NCH, 12)),
            dma((NCH, 12)),
            dma((NCH,)),
            dma((NCH,)),
            dma((NCH,)),
            dma((NCH,)),
            dma((NCH,)),
            dma((NCH,)),
        ],
        compiler_params=pltpu.CompilerParams(
            collective_id=0, has_side_effects=True, vmem_limit_bytes=48 * 2**20
        ),
        cost_estimate=pl.CostEstimate(flops=flops, bytes_accessed=moved, transcendentals=0),
    )(
        xe[0], xw[0], rte[0].T, rtw[0].T, afe[0].T, afw[0].T, gain,
        wg[0], wu[0], wd[0], scales[0],
    )
    return outs[0][None], outs[1][None]


def solution(mesh):
    tokens = P("pipe", "expert", None)
    placed = (tokens,) * 6 + (
        P("pipe", None),
        P("pipe", None, "expert"),
        P("pipe", None, "expert"),
        P("pipe", "expert", None),
        P("pipe", None, None),
    )
    return jax.shard_map(
        functools.partial(body, (mesh.shape["pipe"], mesh.shape["expert"])),
        mesh=mesh,
        in_specs=placed,
        out_specs=(tokens, tokens),
        check_vma=False,
    )
```

```python
import functools
import jax
import jax.numpy as jnp
from jax import lax
from jax.experimental import pallas as pl
from jax.experimental.pallas import tpu as pltpu
from jax.sharding import PartitionSpec as P

CAP = 4
NX, NY = 4, 2
NJ = NX * NY
NCH = 4
F32, BF16, I32 = jnp.float32, jnp.bfloat16, jnp.int32
MESH = pl.DeviceIdType.MESH
route_scale = 2.5


def cut(total, num, den):
    return (total * num // den) // 128 * 128


def kernel(
    np_, nz, d, tok, nf,
    xe, xw, rte, rtw, afe, afw, gain, wg, wu, wd, scales,
    oute, outw,
    X, RP, RR, AP, W, WD, GS, T1, T2, PK, Q, G, H, OY, YR, PF, SR, B, C, F, SP, OUT,
    s_loc, s_out, s_rt, r_rt, s_wd, r_wd, s_a, r_a, s_g, r_g, s_h, r_h, s_y, r_y, s_b, r_b, s_f, r_f,
):
    oc = d // NJ
    qc = d // NX
    mr = nz * NJ * 2
    blk = 2 * nz
    half = NX * blk
    ca = cut(d, 5, 9)
    qa = max(cut(d, 2, 9), 128)
    p = lax.axis_index("pipe")
    e = lax.axis_index("expert")
    z = e // NJ
    j = e % NJ
    y = j // NX
    x = j % NX
    base = z * NJ
    xr = (x + 1) % NX
    xl = (x + NX - 1) % NX
    x2 = (x + 2) % NX
    yo = 1 - y
    dev_r = (p, base + y * NX + xr)
    dev_l = (p, base + y * NX + xl)
    dev_y = (p, base + yo * NX + x)
    pn = (p + 1) % np_
    pp = (p + np_ - 1) % np_

    def rc(src, dst, ss, rs, dev):
        return pltpu.make_async_remote_copy(
            src_ref=src, dst_ref=dst, send_sem=ss, recv_sem=rs, device_id=dev, device_id_type=MESH
        )

    def drain(ref, sem):
        pltpu.make_async_copy(ref, ref, sem).wait()

    def qcol(q):
        return pl.ds(pl.multiple_of(q * qc, 128), qc)

    def on_row(send):
        for k in (1, 3, 2):
            t = (x + k) % NX
            send(t, (p, base + y * NX + t))

    local = [
        pltpu.make_async_copy(xe, X.at[0], s_loc.at[0]),
        pltpu.make_async_copy(xw, X.at[1], s_loc.at[1]),
        pltpu.make_async_copy(wg, W.at[:, pl.ds(0, nf)], s_loc.at[2]),
        pltpu.make_async_copy(wu, W.at[:, pl.ds(nf, nf)], s_loc.at[3]),
        pltpu.make_async_copy(
            wd.at[:, qcol(x)], WD.at[pl.ds(pl.multiple_of(x * nf, 128), nf)], s_loc.at[4]
        ),
    ]
    for c in local:
        c.start()

    bar = pltpu.get_barrier_semaphore()

    def greet_z(k, carry):
        zz = (z + k) % nz
        pl.semaphore_signal(bar, inc=1, device_id=(pn, zz * NJ + j), device_id_type=MESH)
        pl.semaphore_signal(bar, inc=1, device_id=(pp, zz * NJ + j), device_id_type=MESH)
        return carry

    lax.fori_loop(0, nz, greet_z, 0)

    def greet_own(k, carry):
        pl.semaphore_signal(
            bar, inc=1, device_id=(p, (z + k) % nz * NJ + j), device_id_type=MESH
        )
        return carry

    lax.fori_loop(1, nz, greet_own, 0)

    def greet(t, dev):
        pl.semaphore_signal(bar, inc=1, device_id=dev, device_id_type=MESH)

    on_row(greet)
    greet(x, dev_y)

    RP[...] = jnp.full(RP.shape, -1, I32)
    RP[0, :, 0:tok] = rte[...]
    RP[1, :, 0:tok] = rtw[...]
    AP[...] = jnp.full(AP.shape, 1.0, F32)
    AP[0, :, 0:tok] = afe[...]
    AP[1, :, 0:tok] = afw[...]

    pl.semaphore_wait(bar, 2 * nz + (nz - 1) + NX)

    rt_e = rc(RP.at[0], RR.at[0], s_rt.at[0], r_rt.at[0], (pp, e))
    rt_w = rc(RP.at[1], RR.at[1], s_rt.at[1], r_rt.at[1], (pn, e))
    rt_e.start()
    rt_w.start()

    def send_wd(t, dev):
        rc(
            wd.at[:, qcol(t)],
            WD.at[pl.ds(pl.multiple_of(x * nf, 128), nf)],
            s_wd.at[0],
            r_wd.at[0],
            dev,
        ).start()

    on_row(send_wd)

    def iot(shape, dim):
        return lax.broadcasted_iota(I32, shape, dim)

    lanes = RP.shape[2]
    row = iot((mr, lanes), 0)
    zrow = row // (2 * NJ)
    orow = (row // 2) % NJ
    crow = row % 2
    before = (iot((lanes, lanes), 0) < iot((lanes, lanes), 1)).astype(F32).astype(BF16)

    def slots(rt):
        chosen = jnp.zeros((mr, lanes), F32)
        for k in range(rt.shape[0]):
            chosen = chosen + jnp.where(rt[k : k + 1, :] == zrow, 1.0, 0.0)
        rank = jnp.dot(chosen.astype(BF16), before, preferred_element_type=F32)
        return chosen, rank.astype(I32)

    local[0].wait()
    local[1].wait()
    rt_e.wait_recv()
    rt_w.wait_recv()

    def stage_a(c):
        m, k = c // 2, c % 2
        chosen, rank = slots(RR[m])
        pick = jnp.where((chosen > 0.0) & (rank == 2 * k + crow), 1.0, 0.0)
        acc = jnp.zeros((mr, oc), F32)
        for o in range(NJ):
            part = jnp.where(orow == o, pick, 0.0).astype(BF16)[:, 0:tok]
            acc = acc + jnp.dot(part, X[m, :, o * oc : (o + 1) * oc], preferred_element_type=F32)
        PK[c] = acc.astype(BF16)

    def send_a(c):
        m = c // 2
        to = (p + 1 + m * (np_ - 2)) % np_

        def send(i, carry):
            t = (z + i) % nz
            rc(
                PK.at[c, pl.ds(pl.multiple_of(t * 2 * NJ, 16), 2 * NJ)],
                Q.at[c, pl.ds(pl.multiple_of(z * 2 * NJ, 16), 2 * NJ)],
                s_a.at[c],
                r_a.at[c],
                (to, t * NJ + j),
            ).start()
            return carry

        lax.fori_loop(0, nz, send, 0)

    def blk_of(c, yy, xx, lo, hi):
        return G.at[c, yy * NX + xx, :, pl.ds(lo, hi - lo)]

    def msg(c, n, yy, xx, lo, hi, dev):
        ref = blk_of(c, yy, xx, lo, hi)
        return rc(ref, ref, s_g.at[c, n], r_g.at[c, n], dev)

    def level0(c):
        return (
            msg(c, 0, y, x, 0, d, dev_r),
            msg(c, 1, y, x, 0, d, dev_l),
            msg(c, 2, y, x, 0, d, dev_y),
        )

    def level1(c):
        return (
            msg(c, 3, y, xl, 0, ca, dev_r),
            msg(c, 4, y, xr, ca, d, dev_l),
            msg(c, 5, y, xl, ca, d, dev_y),
            msg(c, 6, y, xr, ca, d, dev_y),
            msg(c, 7, yo, x, 0, ca, dev_r),
            msg(c, 8, yo, x, 0, ca, dev_l),
        )

    def level2(c):
        return (
            msg(c, 9, y, x2, ca, d, dev_y),
            msg(c, 10, yo, xl, 0, qa, dev_r),
            msg(c, 11, yo, xr, qa, ca, dev_l),
        )

    def stage_b(c):
        drain(Q.at[c], r_a.at[c])
        u = jnp.dot(T1[...], Q[c], preferred_element_type=F32)
        sq = jnp.zeros((blk, 1), F32)
        for o in range(NJ):
            v = u[o * blk : (o + 1) * blk]
            sq = sq + jnp.sum(v * v, axis=1, keepdims=True)
        inv = lax.rsqrt(sq / d + 1e-6)
        for o in range(NJ):
            v = u[o * blk : (o + 1) * blk]
            G[c, j, :, o * oc : (o + 1) * oc] = (v * inv * GS[:, o * oc : (o + 1) * oc]).astype(BF16)
        for s in level0(c):
            s.start()

    def stage_l1(c):
        a, b, w = level0(c)
        m3, m4, m5, m6, m7, m8 = level1(c)
        a.wait_recv()
        m3.start()
        m5.start()
        b.wait_recv()
        m4.start()
        m6.start()
        w.wait_recv()
        m7.start()
        m8.start()

    def stage_l2(c):
        _, m4, _, _, m7, m8 = level1(c)
        m9, m10, m11 = level2(c)
        m4.wait_recv()
        m9.start()
        m7.wait_recv()
        m10.start()
        m8.wait_recv()
        m11.start()

    def stage_d(c):
        m3, _, m5, m6, _, _ = level1(c)
        for s in (m3, m5, m6) + level2(c):
            s.wait_recv()
        kb = d // 7 if d % (7 * 128) == 0 else 128

        def step(i, acc):
            cols = pl.ds(pl.multiple_of(i * kb, 128), kb)
            rows = G[c, :, :, cols].reshape(NJ * blk, kb)
            return acc + jnp.dot(rows, W[cols, :], preferred_element_type=F32)

        acc = lax.fori_loop(0, d // kb, step, jnp.zeros((NJ * blk, 2 * nf), F32))
        gate, up = acc[:, 0:nf], acc[:, nf : 2 * nf]
        H[c, x] = (gate / (1.0 + jnp.exp(-gate)) * up).astype(BF16)

        def send(t, dev):
            rc(H.at[c, x], H.at[c, x], s_h.at[c], r_h.at[c], dev).start()

        on_row(send)

    def to_y(c):
        return rc(OY.at[c], YR.at[c], s_y.at[c], r_y.at[c], dev_y)

    def stage_e(c):
        drain(H.at[c, pl.ds(0, NX - 1)], r_h.at[c])

        def down(yy):
            rows = pl.ds(pl.multiple_of(yy * half, half), half)
            hid = jnp.concatenate([H[c, i, rows] for i in range(NX)], axis=1)
            return jnp.dot(hid, WD[...], preferred_element_type=F32)

        OY[c] = down(yo).astype(BF16)
        to_y(c).start()
        PF[c] = down(y)

    def stage_s(c):
        to_y(c).wait_recv()
        SR[c] = (PF[c] + YR[c].astype(F32)).astype(BF16)

        def octant(h):
            return pl.ds(pl.multiple_of((2 * x + h) * blk, blk), blk)

        def rows(t):
            return pl.ds(pl.multiple_of(t * blk, blk), blk)

        for h in range(2):
            B[c, octant(h)] = SR[c, rows(x), h * oc : (h + 1) * oc]

        def send(t, dev):
            for h in range(2):
                rc(
                    SR.at[c, rows(t), pl.ds(h * oc, oc)],
                    B.at[c, octant(h)],
                    s_b.at[c],
                    r_b.at[c],
                    dev,
                ).start()

        on_row(send)

    def stage_f(c):
        drain(B.at[c, pl.ds(0, 2 * (NX - 1) * blk)], r_b.at[c])
        C[c] = jnp.dot(T2[...], B[c], preferred_element_type=F32).astype(BF16)
        own = pl.ds(pl.multiple_of(z * 2 * NJ, 16), 2 * NJ)
        F[c, own] = C[c, own]

        def send(i, carry):
            t = (z + i) % nz
            rc(
                C.at[c, pl.ds(pl.multiple_of(t * 2 * NJ, 16), 2 * NJ)],
                F.at[c, own],
                s_f.at[c],
                r_f.at[c],
                (p, t * NJ + j),
            ).start()
            return carry

        lax.fori_loop(1, nz, send, 0)

    def spread(m):
        rt = RP[m]
        af = AP[m]
        share = route_scale * af / jnp.sum(af, axis=0, keepdims=True)
        weight = jnp.zeros((mr, lanes), F32)
        for k in range(rt.shape[0]):
            weight = weight + jnp.where(rt[k : k + 1, :] == zrow, share[k : k + 1, :], 0.0)
        chosen, rank = slots(rt)
        olane = (iot((tok, mr), 1) // 2) % NJ
        for k in range(2):
            s = jnp.where((chosen > 0.0) & (rank == 2 * k + crow), weight, 0.0)
            s = jnp.transpose(s)[0:tok]
            hi = s.astype(BF16).astype(F32)
            lo = s - hi
            for h, v in ((0, hi), (1, lo)):
                for o in range(NJ):
                    SP[m, h, o * tok : (o + 1) * tok, k * mr : (k + 1) * mr] = jnp.where(
                        olane == o, v, 0.0
                    ).astype(BF16)

    def stage_g(m):
        for k in range(2):
            drain(F.at[2 * m + k, pl.ds(0, (nz - 1) * 2 * NJ)], r_f.at[2 * m + k])
        rows = F[pl.ds(2 * m, 2)].reshape(2 * mr, oc)
        res = jnp.dot(SP[m, 0], rows, preferred_element_type=F32)
        res = res + jnp.dot(SP[m, 1], rows, preferred_element_type=F32)
        for o in range(NJ):
            OUT[m, :, o * oc : (o + 1) * oc] = res[o * tok : (o + 1) * tok].astype(BF16)

    def pack_loop(c, carry):
        stage_a(c)
        pl.when(c == 0)(lambda: send_a(c))
        return carry

    lax.fori_loop(0, NCH, pack_loop, 0)
    r_ = iot((mr, mr), 0)
    c_ = iot((mr, mr), 1)
    hit = (
        (r_ // blk == (c_ // 2) % NJ) & ((r_ // 2) % nz == c_ // (2 * NJ)) & (r_ % 2 == c_ % 2)
    )
    T1[...] = hit.astype(F32).astype(BF16)
    hit2 = (
        (c_ // blk == (r_ // 2) % NJ) & ((c_ // 2) % nz == r_ // (2 * NJ)) & (r_ % 2 == c_ % 2)
    )
    T2[...] = hit2.astype(F32).astype(BF16)

    def gain_block(k, carry):
        s = scales[z, k]
        f = jnp.where(s > 0, 2.0, jnp.where(s < 0, 0.5, 1.0)).astype(F32)
        cols = pl.ds(pl.multiple_of(k * 128, 128), 128)
        GS[:, cols] = gain[:, cols] * f
        return carry

    lax.fori_loop(0, d // 128, gain_block, 0)

    spread(0)
    spread(1)

    def main(it, carry):
        def when(lag, f):
            c = it - lag
            pl.when((c >= 0) & (c < NCH))(lambda: f(c))

        def next_a(c):
            drain(PK.at[c], s_a.at[c])
            send_a(c + 1)

        pl.when(it < NCH - 1)(lambda: next_a(it))
        when(0, stage_b)
        when(1, stage_l1)
        when(2, stage_l2)

        @pl.when(it == 3)
        def _():
            local[2].wait()
            local[3].wait()
            local[4].wait()
            drain(WD.at[pl.ds(0, (NX - 1) * nf)], r_wd.at[0])

        when(3, stage_d)
        when(4, stage_e)
        when(5, stage_s)
        when(6, stage_f)

        @pl.when(it == 8)
        def _():
            stage_g(0)
            pltpu.make_async_copy(OUT.at[0], oute, s_out.at[0]).start()

        @pl.when(it == 10)
        def _():
            stage_g(1)
            pltpu.make_async_copy(OUT.at[1], outw, s_out.at[1]).start()

        return carry

    lax.fori_loop(0, 11, main, 0)

    rt_e.wait_send()
    rt_w.wait_send()
    drain(WD.at[pl.ds(0, (NX - 1) * nf)], s_wd.at[0])

    def finish(c, carry):
        for s in level0(c) + level1(c) + level2(c):
            s.wait_send()
        drain(H.at[c, pl.ds(0, NX - 1)], s_h.at[c])
        to_y(c).wait_send()
        drain(B.at[c, pl.ds(0, 2 * (NX - 1) * blk)], s_b.at[c])
        drain(C.at[c, pl.ds(0, (nz - 1) * 2 * NJ)], s_f.at[c])
        return carry

    lax.fori_loop(0, NCH, finish, 0)
    drain(PK.at[NCH - 1], s_a.at[NCH - 1])
    pltpu.make_async_copy(OUT.at[0], oute, s_out.at[0]).wait()
    pltpu.make_async_copy(OUT.at[1], outw, s_out.at[1]).wait()


def body(mesh_shape, xe, xw, rte, rtw, afe, afw, gain, wg, wu, wd, scales):
    np_, ne = mesh_shape
    nz = ne // NJ
    _, tok, d = xe.shape
    nf = wg.shape[2]
    oc = d // NJ
    mr = nz * NJ * 2
    blk = 2 * nz
    top = rte.shape[2]
    any_, vm = pl.BlockSpec(memory_space=pl.ANY), pl.BlockSpec(memory_space=pltpu.VMEM)
    dma = pltpu.SemaphoreType.DMA
    flops = 2 * NCH * NJ * blk * d * 3 * nf
    moved = 2 * 2 * (4 * tok * d + 3 * d * nf)
    outs = pl.pallas_call(
        functools.partial(kernel, np_, nz, d, tok, nf),
        out_shape=[jax.ShapeDtypeStruct((tok, d), BF16)] * 2,
        in_specs=[any_, any_, vm, vm, vm, vm, vm, any_, any_, any_]
        + [pl.BlockSpec(memory_space=pltpu.SMEM)],
        out_specs=[any_, any_],
        scratch_shapes=[
            pltpu.VMEM((2, tok, d), BF16),
            pltpu.VMEM((2, top, 128), I32),
            pltpu.VMEM((2, top, 128), I32),
            pltpu.VMEM((2, top, 128), F32),
            pltpu.VMEM((d, 2 * nf), BF16),
            pltpu.VMEM((NX * nf, d // NX), BF16),
            pltpu.VMEM((1, d), F32),
            pltpu.VMEM((mr, mr), BF16),
            pltpu.VMEM((mr, mr), BF16),
            pltpu.VMEM((NCH, mr, oc), BF16),
            pltpu.VMEM((NCH, mr, oc), BF16),
            pltpu.VMEM((NCH, NJ, blk, d), BF16),
            pltpu.VMEM((NCH, NX, NJ * blk, nf), BF16),
            pltpu.VMEM((NCH, NX * blk, d // NX), BF16),
            pltpu.VMEM((NCH, NX * blk, d // NX), BF16),
            pltpu.VMEM((NCH, NX * blk, d // NX), F32),
            pltpu.VMEM((NCH, NX * blk, d // NX), BF16),
            pltpu.VMEM((NCH, NJ * blk, oc), BF16),
            pltpu.VMEM((NCH, mr, oc), BF16),
            pltpu.VMEM((NCH, mr, oc), BF16),
            pltpu.VMEM((2, 2, NJ * tok, 2 * mr), BF16),
            pltpu.VMEM((2, tok, d), BF16),
            dma((5,)),
            dma((2,)),
            dma((2,)),
            dma((2,)),
            dma((1,)),
            dma((1,)),
            dma((NCH,)),
            dma((NCH,)),
            dma((NCH, 12)),
            dma((NCH, 12)),
            dma((NCH,)),
            dma((NCH,)),
            dma((NCH,)),
            dma((NCH,)),
            dma((NCH,)),
            dma((NCH,)),
            dma((NCH,)),
            dma((NCH,)),
        ],
        compiler_params=pltpu.CompilerParams(
            collective_id=0, has_side_effects=True, vmem_limit_bytes=63 * 2**20
        ),
        cost_estimate=pl.CostEstimate(flops=flops, bytes_accessed=moved, transcendentals=0),
    )(
        xe[0], xw[0], rte[0].T, rtw[0].T, afe[0].T, afw[0].T, gain,
        wg[0], wu[0], wd[0], scales[0],
    )
    return outs[0][None], outs[1][None]


def solution(mesh):
    tokens = P("pipe", "expert", None)
    placed = (tokens,) * 6 + (
        P("pipe", None),
        P("pipe", None, "expert"),
        P("pipe", None, "expert"),
        P("pipe", "expert", None),
        P("pipe", None, None),
    )
    return jax.shard_map(
        functools.partial(body, (mesh.shape["pipe"], mesh.shape["expert"])),
        mesh=mesh,
        in_specs=placed,
        out_specs=(tokens, tokens),
        check_vma=False,
    )
```

```python
import functools
import jax
import jax.numpy as jnp
from jax import lax
from jax.experimental import pallas as pl
from jax.experimental.pallas import tpu as pltpu
from jax.sharding import PartitionSpec as P

CAP = 4
NX, NY = 4, 2
NJ = NX * NY
NCH = 4
F32, BF16, I32 = jnp.float32, jnp.bfloat16, jnp.int32
MESH = pl.DeviceIdType.MESH
route_scale = 2.5


def cut(total, num, den):
    return (total * num // den) // 128 * 128


def kernel(
    np_, nz, d, tok, nf,
    xe, xw, rte, rtw, afe, afw, gain, wg, wu, wd, scales,
    oute, outw,
    X, RP, RR, AP, W, WD, GS, T1, T2, PK, Q, G, H, OY, YR, PF, SR, B, C, F, SP, OUT,
    s_loc, s_out, s_rt, r_rt, s_wd, r_wd, s_a, r_a, s_g, r_g, s_h, r_h, s_y, r_y, s_b, r_b, s_f, r_f,
):
    oc = d // NJ
    qc = d // NX
    mr = nz * NJ * 2
    blk = 2 * nz
    half = NX * blk
    ca = cut(d, 5, 9)
    qa = max(cut(d, 2, 9), 128)
    p = lax.axis_index("pipe")
    e = lax.axis_index("expert")
    z = e // NJ
    j = e % NJ
    y = j // NX
    x = j % NX
    base = z * NJ
    xr = (x + 1) % NX
    xl = (x + NX - 1) % NX
    x2 = (x + 2) % NX
    yo = 1 - y
    dev_r = (p, base + y * NX + xr)
    dev_l = (p, base + y * NX + xl)
    dev_y = (p, base + yo * NX + x)
    pn = (p + 1) % np_
    pp = (p + np_ - 1) % np_

    def rc(src, dst, ss, rs, dev):
        return pltpu.make_async_remote_copy(
            src_ref=src, dst_ref=dst, send_sem=ss, recv_sem=rs, device_id=dev, device_id_type=MESH
        )

    def drain(ref, sem):
        pltpu.make_async_copy(ref, ref, sem).wait()

    def qcol(q):
        return pl.ds(pl.multiple_of(q * qc, 128), qc)

    def on_row(send):
        for k in (1, 3, 2):
            t = (x + k) % NX
            send(t, (p, base + y * NX + t))

    local = [
        pltpu.make_async_copy(xe, X.at[0], s_loc.at[0]),
        pltpu.make_async_copy(xw, X.at[1], s_loc.at[1]),
        pltpu.make_async_copy(wg, W.at[:, pl.ds(0, nf)], s_loc.at[2]),
        pltpu.make_async_copy(wu, W.at[:, pl.ds(nf, nf)], s_loc.at[3]),
        pltpu.make_async_copy(
            wd.at[:, qcol(x)], WD.at[pl.ds(pl.multiple_of(x * nf, 128), nf)], s_loc.at[4]
        ),
    ]
    for c in local:
        c.start()

    bar = pltpu.get_barrier_semaphore()

    def greet_z(k, carry):
        zz = (z + k) % nz
        pl.semaphore_signal(bar, inc=1, device_id=(pn, zz * NJ + j), device_id_type=MESH)
        pl.semaphore_signal(bar, inc=1, device_id=(pp, zz * NJ + j), device_id_type=MESH)
        return carry

    lax.fori_loop(0, nz, greet_z, 0)

    def greet_own(k, carry):
        pl.semaphore_signal(
            bar, inc=1, device_id=(p, (z + k) % nz * NJ + j), device_id_type=MESH
        )
        return carry

    lax.fori_loop(1, nz, greet_own, 0)

    def greet(t, dev):
        pl.semaphore_signal(bar, inc=1, device_id=dev, device_id_type=MESH)

    on_row(greet)
    greet(x, dev_y)

    RP[...] = jnp.full(RP.shape, -1, I32)
    RP[0, :, 0:tok] = rte[...]
    RP[1, :, 0:tok] = rtw[...]
    AP[...] = jnp.full(AP.shape, 1.0, F32)
    AP[0, :, 0:tok] = afe[...]
    AP[1, :, 0:tok] = afw[...]

    pl.semaphore_wait(bar, 2 * nz + (nz - 1) + NX)

    rt_e = rc(RP.at[0], RR.at[0], s_rt.at[0], r_rt.at[0], (pp, e))
    rt_w = rc(RP.at[1], RR.at[1], s_rt.at[1], r_rt.at[1], (pn, e))
    rt_e.start()
    rt_w.start()

    def send_wd(t, dev):
        rc(
            wd.at[:, qcol(t)],
            WD.at[pl.ds(pl.multiple_of(x * nf, 128), nf)],
            s_wd.at[0],
            r_wd.at[0],
            dev,
        ).start()

    on_row(send_wd)

    def iot(shape, dim):
        return lax.broadcasted_iota(I32, shape, dim)

    lanes = RP.shape[2]
    row = iot((mr, lanes), 0)
    zrow = row // (2 * NJ)
    orow = (row // 2) % NJ
    crow = row % 2
    before = (iot((lanes, lanes), 0) < iot((lanes, lanes), 1)).astype(F32).astype(BF16)

    def slots(rt):
        chosen = jnp.zeros((mr, lanes), F32)
        for k in range(rt.shape[0]):
            chosen = chosen + jnp.where(rt[k : k + 1, :] == zrow, 1.0, 0.0)
        rank = jnp.dot(chosen.astype(BF16), before, preferred_element_type=F32)
        return chosen, rank.astype(I32)

    local[0].wait()
    local[1].wait()
    rt_e.wait_recv()
    rt_w.wait_recv()

    def stage_a(c):
        m, k = c // 2, c % 2
        chosen, rank = slots(RR[m])
        pick = jnp.where((chosen > 0.0) & (rank == 2 * k + crow), 1.0, 0.0)
        acc = jnp.zeros((mr, oc), F32)
        for o in range(NJ):
            part = jnp.where(orow == o, pick, 0.0).astype(BF16)[:, 0:tok]
            acc = acc + jnp.dot(part, X[m, :, o * oc : (o + 1) * oc], preferred_element_type=F32)
        PK[c] = acc.astype(BF16)

    def send_a(c):
        m = c // 2
        to = (p + 1 + m * (np_ - 2)) % np_

        def send(i, carry):
            t = (z + i) % nz
            rc(
                PK.at[c, pl.ds(pl.multiple_of(t * 2 * NJ, 16), 2 * NJ)],
                Q.at[c, pl.ds(pl.multiple_of(z * 2 * NJ, 16), 2 * NJ)],
                s_a.at[c],
                r_a.at[c],
                (to, t * NJ + j),
            ).start()
            return carry

        lax.fori_loop(0, nz, send, 0)

    def blk_of(c, yy, xx, lo, hi):
        return G.at[c, yy * NX + xx, :, pl.ds(lo, hi - lo)]

    def msg(c, n, yy, xx, lo, hi, dev):
        ref = blk_of(c, yy, xx, lo, hi)
        return rc(ref, ref, s_g.at[c, n], r_g.at[c, n], dev)

    def level0(c):
        return (
            msg(c, 0, y, x, 0, d, dev_r),
            msg(c, 1, y, x, 0, d, dev_l),
            msg(c, 2, y, x, 0, d, dev_y),
        )

    def level1(c):
        return (
            msg(c, 3, y, xl, 0, ca, dev_r),
            msg(c, 4, y, xr, ca, d, dev_l),
            msg(c, 5, y, xl, ca, d, dev_y),
            msg(c, 6, y, xr, ca, d, dev_y),
            msg(c, 7, yo, x, 0, ca, dev_r),
            msg(c, 8, yo, x, 0, ca, dev_l),
        )

    def level2(c):
        return (
            msg(c, 9, y, x2, ca, d, dev_y),
            msg(c, 10, yo, xl, 0, qa, dev_r),
            msg(c, 11, yo, xr, qa, ca, dev_l),
        )

    def stage_b(c):
        drain(Q.at[c], r_a.at[c])
        u = jnp.dot(T1[...], Q[c], preferred_element_type=F32)
        sq = jnp.zeros((blk, 1), F32)
        for o in range(NJ):
            v = u[o * blk : (o + 1) * blk]
            sq = sq + jnp.sum(v * v, axis=1, keepdims=True)
        inv = lax.rsqrt(sq / d + 1e-6)
        for o in range(NJ):
            v = u[o * blk : (o + 1) * blk]
            G[c, j, :, o * oc : (o + 1) * oc] = (v * inv * GS[:, o * oc : (o + 1) * oc]).astype(BF16)
        for s in level0(c)[::-1]:
            s.start()

    def stage_l1(c):
        a, b, w = level0(c)
        m3, m4, m5, m6, m7, m8 = level1(c)
        a.wait_recv()
        m3.start()
        m5.start()
        b.wait_recv()
        m4.start()
        m6.start()
        w.wait_recv()
        m7.start()
        m8.start()

    def stage_l2(c):
        _, m4, _, _, m7, m8 = level1(c)
        m9, m10, m11 = level2(c)
        m4.wait_recv()
        m9.start()
        m7.wait_recv()
        m10.start()
        m8.wait_recv()
        m11.start()

    def stage_d(c):
        m3, _, m5, m6, _, _ = level1(c)
        for s in (m3, m5, m6) + level2(c):
            s.wait_recv()
        kb = d // 7 if d % (7 * 128) == 0 else 128

        def step(i, acc):
            cols = pl.ds(pl.multiple_of(i * kb, 128), kb)
            rows = G[c, :, :, cols].reshape(NJ * blk, kb)
            return acc + jnp.dot(rows, W[cols, :], preferred_element_type=F32)

        acc = lax.fori_loop(0, d // kb, step, jnp.zeros((NJ * blk, 2 * nf), F32))
        gate, up = acc[:, 0:nf], acc[:, nf : 2 * nf]
        H[c, x] = (gate / (1.0 + jnp.exp(-gate)) * up).astype(BF16)

        def send(t, dev):
            rc(H.at[c, x], H.at[c, x], s_h.at[c], r_h.at[c], dev).start()

        on_row(send)

    def to_y(c):
        return rc(OY.at[c], YR.at[c], s_y.at[c], r_y.at[c], dev_y)

    def stage_e(c):
        drain(H.at[c, pl.ds(0, NX - 1)], r_h.at[c])

        def down(yy):
            rows = pl.ds(pl.multiple_of(yy * half, half), half)
            hid = jnp.concatenate([H[c, i, rows] for i in range(NX)], axis=1)
            return jnp.dot(hid, WD[...], preferred_element_type=F32)

        OY[c] = down(yo).astype(BF16)
        to_y(c).start()
        PF[c] = down(y)

    def stage_s(c):
        to_y(c).wait_recv()
        SR[c] = (PF[c] + YR[c].astype(F32)).astype(BF16)

        def octant(h):
            return pl.ds(pl.multiple_of((2 * x + h) * blk, blk), blk)

        def rows(t):
            return pl.ds(pl.multiple_of(t * blk, blk), blk)

        for h in range(2):
            B[c, octant(h)] = SR[c, rows(x), h * oc : (h + 1) * oc]

        def send(t, dev):
            for h in range(2):
                rc(
                    SR.at[c, rows(t), pl.ds(h * oc, oc)],
                    B.at[c, octant(h)],
                    s_b.at[c],
                    r_b.at[c],
                    dev,
                ).start()

        on_row(send)

    def stage_f(c):
        drain(B.at[c, pl.ds(0, 2 * (NX - 1) * blk)], r_b.at[c])
        C[c] = jnp.dot(T2[...], B[c], preferred_element_type=F32).astype(BF16)
        own = pl.ds(pl.multiple_of(z * 2 * NJ, 16), 2 * NJ)
        F[c, own] = C[c, own]

        def send(i, carry):
            t = (z + i) % nz
            rc(
                C.at[c, pl.ds(pl.multiple_of(t * 2 * NJ, 16), 2 * NJ)],
                F.at[c, own],
                s_f.at[c],
                r_f.at[c],
                (p, t * NJ + j),
            ).start()
            return carry

        lax.fori_loop(1, nz, send, 0)

    def spread(m):
        rt = RP[m]
        af = AP[m]
        share = route_scale * af / jnp.sum(af, axis=0, keepdims=True)
        weight = jnp.zeros((mr, lanes), F32)
        for k in range(rt.shape[0]):
            weight = weight + jnp.where(rt[k : k + 1, :] == zrow, share[k : k + 1, :], 0.0)
        chosen, rank = slots(rt)
        olane = (iot((tok, mr), 1) // 2) % NJ
        for k in range(2):
            s = jnp.where((chosen > 0.0) & (rank == 2 * k + crow), weight, 0.0)
            s = jnp.transpose(s)[0:tok]
            hi = s.astype(BF16).astype(F32)
            lo = s - hi
            for h, v in ((0, hi), (1, lo)):
                for o in range(NJ):
                    SP[m, h, o * tok : (o + 1) * tok, k * mr : (k + 1) * mr] = jnp.where(
                        olane == o, v, 0.0
                    ).astype(BF16)

    def stage_g(m):
        for k in range(2):
            drain(F.at[2 * m + k, pl.ds(0, (nz - 1) * 2 * NJ)], r_f.at[2 * m + k])
        rows = F[pl.ds(2 * m, 2)].reshape(2 * mr, oc)
        res = jnp.dot(SP[m, 0], rows, preferred_element_type=F32)
        res = res + jnp.dot(SP[m, 1], rows, preferred_element_type=F32)
        for o in range(NJ):
            OUT[m, :, o * oc : (o + 1) * oc] = res[o * tok : (o + 1) * tok].astype(BF16)

    def pack_loop(c, carry):
        stage_a(c)
        send_a(c)
        return carry

    lax.fori_loop(0, NCH, pack_loop, 0)
    r_ = iot((mr, mr), 0)
    c_ = iot((mr, mr), 1)
    hit = (
        (r_ // blk == (c_ // 2) % NJ) & ((r_ // 2) % nz == c_ // (2 * NJ)) & (r_ % 2 == c_ % 2)
    )
    T1[...] = hit.astype(F32).astype(BF16)
    hit2 = (
        (c_ // blk == (r_ // 2) % NJ) & ((c_ // 2) % nz == r_ // (2 * NJ)) & (r_ % 2 == c_ % 2)
    )
    T2[...] = hit2.astype(F32).astype(BF16)

    def gain_block(k, carry):
        s = scales[z, k]
        f = jnp.where(s > 0, 2.0, jnp.where(s < 0, 0.5, 1.0)).astype(F32)
        cols = pl.ds(pl.multiple_of(k * 128, 128), 128)
        GS[:, cols] = gain[:, cols] * f
        return carry

    lax.fori_loop(0, d // 128, gain_block, 0)

    spread(0)
    spread(1)

    def main(it, carry):
        def when(lag, f):
            c = it - lag
            pl.when((c >= 0) & (c < NCH))(lambda: f(c))

        when(0, stage_b)
        when(1, stage_l1)
        when(2, stage_l2)

        @pl.when(it == 3)
        def _():
            local[2].wait()
            local[3].wait()
            local[4].wait()
            drain(WD.at[pl.ds(0, (NX - 1) * nf)], r_wd.at[0])

        when(3, stage_d)
        when(4, stage_e)
        when(5, stage_s)
        when(6, stage_f)

        @pl.when(it == 8)
        def _():
            stage_g(0)
            pltpu.make_async_copy(OUT.at[0], oute, s_out.at[0]).start()

        @pl.when(it == 10)
        def _():
            stage_g(1)
            pltpu.make_async_copy(OUT.at[1], outw, s_out.at[1]).start()

        return carry

    lax.fori_loop(0, 11, main, 0)

    rt_e.wait_send()
    rt_w.wait_send()
    drain(WD.at[pl.ds(0, (NX - 1) * nf)], s_wd.at[0])

    def finish(c, carry):
        for s in level0(c) + level1(c) + level2(c):
            s.wait_send()
        drain(H.at[c, pl.ds(0, NX - 1)], s_h.at[c])
        to_y(c).wait_send()
        drain(B.at[c, pl.ds(0, 2 * (NX - 1) * blk)], s_b.at[c])
        drain(C.at[c, pl.ds(0, (nz - 1) * 2 * NJ)], s_f.at[c])
        return carry

    lax.fori_loop(0, NCH, finish, 0)
    for c in range(NCH):
        drain(PK.at[c], s_a.at[c])
    pltpu.make_async_copy(OUT.at[0], oute, s_out.at[0]).wait()
    pltpu.make_async_copy(OUT.at[1], outw, s_out.at[1]).wait()


def body(mesh_shape, xe, xw, rte, rtw, afe, afw, gain, wg, wu, wd, scales):
    np_, ne = mesh_shape
    nz = ne // NJ
    _, tok, d = xe.shape
    nf = wg.shape[2]
    oc = d // NJ
    mr = nz * NJ * 2
    blk = 2 * nz
    top = rte.shape[2]
    any_, vm = pl.BlockSpec(memory_space=pl.ANY), pl.BlockSpec(memory_space=pltpu.VMEM)
    dma = pltpu.SemaphoreType.DMA
    flops = 2 * NCH * NJ * blk * d * 3 * nf
    moved = 2 * 2 * (4 * tok * d + 3 * d * nf)
    outs = pl.pallas_call(
        functools.partial(kernel, np_, nz, d, tok, nf),
        out_shape=[jax.ShapeDtypeStruct((tok, d), BF16)] * 2,
        in_specs=[any_, any_, vm, vm, vm, vm, vm, any_, any_, any_]
        + [pl.BlockSpec(memory_space=pltpu.SMEM)],
        out_specs=[any_, any_],
        scratch_shapes=[
            pltpu.VMEM((2, tok, d), BF16),
            pltpu.VMEM((2, top, 128), I32),
            pltpu.VMEM((2, top, 128), I32),
            pltpu.VMEM((2, top, 128), F32),
            pltpu.VMEM((d, 2 * nf), BF16),
            pltpu.VMEM((NX * nf, d // NX), BF16),
            pltpu.VMEM((1, d), F32),
            pltpu.VMEM((mr, mr), BF16),
            pltpu.VMEM((mr, mr), BF16),
            pltpu.VMEM((NCH, mr, oc), BF16),
            pltpu.VMEM((NCH, mr, oc), BF16),
            pltpu.VMEM((NCH, NJ, blk, d), BF16),
            pltpu.VMEM((NCH, NX, NJ * blk, nf), BF16),
            pltpu.VMEM((NCH, NX * blk, d // NX), BF16),
            pltpu.VMEM((NCH, NX * blk, d // NX), BF16),
            pltpu.VMEM((NCH, NX * blk, d // NX), F32),
            pltpu.VMEM((NCH, NX * blk, d // NX), BF16),
            pltpu.VMEM((NCH, NJ * blk, oc), BF16),
            pltpu.VMEM((NCH, mr, oc), BF16),
            pltpu.VMEM((NCH, mr, oc), BF16),
            pltpu.VMEM((2, 2, NJ * tok, 2 * mr), BF16),
            pltpu.VMEM((2, tok, d), BF16),
            dma((5,)),
            dma((2,)),
            dma((2,)),
            dma((2,)),
            dma((1,)),
            dma((1,)),
            dma((NCH,)),
            dma((NCH,)),
            dma((NCH, 12)),
            dma((NCH, 12)),
            dma((NCH,)),
            dma((NCH,)),
            dma((NCH,)),
            dma((NCH,)),
            dma((NCH,)),
            dma((NCH,)),
            dma((NCH,)),
            dma((NCH,)),
        ],
        compiler_params=pltpu.CompilerParams(
            collective_id=0, has_side_effects=True, vmem_limit_bytes=63 * 2**20
        ),
        cost_estimate=pl.CostEstimate(flops=flops, bytes_accessed=moved, transcendentals=0),
    )(
        xe[0], xw[0], rte[0].T, rtw[0].T, afe[0].T, afw[0].T, gain,
        wg[0], wu[0], wd[0], scales[0],
    )
    return outs[0][None], outs[1][None]


def solution(mesh):
    tokens = P("pipe", "expert", None)
    placed = (tokens,) * 6 + (
        P("pipe", None),
        P("pipe", None, "expert"),
        P("pipe", None, "expert"),
        P("pipe", "expert", None),
        P("pipe", None, None),
    )
    return jax.shard_map(
        functools.partial(body, (mesh.shape["pipe"], mesh.shape["expert"])),
        mesh=mesh,
        in_specs=placed,
        out_specs=(tokens, tokens),
        check_vma=False,
    )
```

```python
import functools
import jax
import jax.numpy as jnp
from jax import lax
from jax.experimental import pallas as pl
from jax.experimental.pallas import tpu as pltpu
from jax.sharding import PartitionSpec as P

CAP = 4
NX, NY = 4, 2
NJ = NX * NY
NCH = 4
F32, BF16, I32 = jnp.float32, jnp.bfloat16, jnp.int32
MESH = pl.DeviceIdType.MESH
route_scale = 2.5


def cut(total, num, den):
    return (total * num // den) // 128 * 128


def kernel(
    np_, nz, d, tok, nf,
    xe, xw, rte, rtw, afe, afw, gain_in, wg, wu, wd, scales,
    oute, outw,
    RS, AS, gain, X, RP, RR, AP, W, WD, GS, T1, T2, PK, Q, G, H, OY, YR, PF, SR, B, C, F, SP, OUT,
    s_small, s_loc, s_out, s_rt, r_rt, s_wd, r_wd, s_a, r_a, s_g, r_g, s_h, r_h, s_y, r_y, s_b, r_b, s_f, r_f,
):
    oc = d // NJ
    qc = d // NX
    mr = nz * NJ * 2
    blk = 2 * nz
    half = NX * blk
    ca = cut(d, 5, 9)
    qa = max(cut(d, 2, 9), 128)
    p = lax.axis_index("pipe")
    e = lax.axis_index("expert")
    z = e // NJ
    j = e % NJ
    y = j // NX
    x = j % NX
    base = z * NJ
    xr = (x + 1) % NX
    xl = (x + NX - 1) % NX
    x2 = (x + 2) % NX
    yo = 1 - y
    dev_r = (p, base + y * NX + xr)
    dev_l = (p, base + y * NX + xl)
    dev_y = (p, base + yo * NX + x)
    pn = (p + 1) % np_
    pp = (p + np_ - 1) % np_

    def rc(src, dst, ss, rs, dev):
        return pltpu.make_async_remote_copy(
            src_ref=src, dst_ref=dst, send_sem=ss, recv_sem=rs, device_id=dev, device_id_type=MESH
        )

    def drain(ref, sem):
        pltpu.make_async_copy(ref, ref, sem).wait()

    def qcol(q):
        return pl.ds(pl.multiple_of(q * qc, 128), qc)

    def on_row(send):
        for k in (1, 3, 2):
            t = (x + k) % NX
            send(t, (p, base + y * NX + t))

    small = [
        pltpu.make_async_copy(rte, RS.at[0], s_small.at[0]),
        pltpu.make_async_copy(rtw, RS.at[1], s_small.at[1]),
        pltpu.make_async_copy(afe, AS.at[0], s_small.at[2]),
        pltpu.make_async_copy(afw, AS.at[1], s_small.at[3]),
        pltpu.make_async_copy(gain_in, gain, s_small.at[4]),
    ]
    for c in small:
        c.start()
    local = [
        pltpu.make_async_copy(xe, X.at[0], s_loc.at[0]),
        pltpu.make_async_copy(xw, X.at[1], s_loc.at[1]),
        pltpu.make_async_copy(wg, W.at[:, pl.ds(0, nf)], s_loc.at[2]),
        pltpu.make_async_copy(wu, W.at[:, pl.ds(nf, nf)], s_loc.at[3]),
        pltpu.make_async_copy(
            wd.at[:, qcol(x)], WD.at[pl.ds(pl.multiple_of(x * nf, 128), nf)], s_loc.at[4]
        ),
    ]
    for c in local:
        c.start()

    bar = pltpu.get_barrier_semaphore()

    def greet_z(k, carry):
        zz = (z + k) % nz
        pl.semaphore_signal(bar, inc=1, device_id=(pn, zz * NJ + j), device_id_type=MESH)
        pl.semaphore_signal(bar, inc=1, device_id=(pp, zz * NJ + j), device_id_type=MESH)
        return carry

    lax.fori_loop(0, nz, greet_z, 0)

    def greet_own(k, carry):
        pl.semaphore_signal(
            bar, inc=1, device_id=(p, (z + k) % nz * NJ + j), device_id_type=MESH
        )
        return carry

    lax.fori_loop(1, nz, greet_own, 0)

    def greet(t, dev):
        pl.semaphore_signal(bar, inc=1, device_id=dev, device_id_type=MESH)

    on_row(greet)
    greet(x, dev_y)

    for c in small:
        c.wait()
    RP[...] = jnp.full(RP.shape, -1, I32)
    RP[0, :, 0:tok] = RS[0]
    RP[1, :, 0:tok] = RS[1]
    AP[...] = jnp.full(AP.shape, 1.0, F32)
    AP[0, :, 0:tok] = AS[0]
    AP[1, :, 0:tok] = AS[1]

    pl.semaphore_wait(bar, 2 * nz + (nz - 1) + NX)

    rt_e = rc(RP.at[0], RR.at[0], s_rt.at[0], r_rt.at[0], (pp, e))
    rt_w = rc(RP.at[1], RR.at[1], s_rt.at[1], r_rt.at[1], (pn, e))
    rt_e.start()
    rt_w.start()

    def send_wd(t, dev):
        rc(
            wd.at[:, qcol(t)],
            WD.at[pl.ds(pl.multiple_of(x * nf, 128), nf)],
            s_wd.at[0],
            r_wd.at[0],
            dev,
        ).start()

    on_row(send_wd)

    def iot(shape, dim):
        return lax.broadcasted_iota(I32, shape, dim)

    lanes = RP.shape[2]
    row = iot((mr, lanes), 0)
    zrow = row // (2 * NJ)
    orow = (row // 2) % NJ
    crow = row % 2
    before = (iot((lanes, lanes), 0) < iot((lanes, lanes), 1)).astype(F32).astype(BF16)

    def slots(rt):
        chosen = jnp.zeros((mr, lanes), F32)
        for k in range(rt.shape[0]):
            chosen = chosen + jnp.where(rt[k : k + 1, :] == zrow, 1.0, 0.0)
        rank = jnp.dot(chosen.astype(BF16), before, preferred_element_type=F32)
        return chosen, rank.astype(I32)

    local[0].wait()
    local[1].wait()
    rt_e.wait_recv()
    rt_w.wait_recv()

    def stage_a(c):
        m, k = c // 2, c % 2
        chosen, rank = slots(RR[m])
        pick = jnp.where((chosen > 0.0) & (rank == 2 * k + crow), 1.0, 0.0)
        acc = jnp.zeros((mr, oc), F32)
        for o in range(NJ):
            part = jnp.where(orow == o, pick, 0.0).astype(BF16)[:, 0:tok]
            acc = acc + jnp.dot(part, X[m, :, o * oc : (o + 1) * oc], preferred_element_type=F32)
        PK[c] = acc.astype(BF16)

    def send_a(c):
        m = c // 2
        to = (p + 1 + m * (np_ - 2)) % np_

        def send(i, carry):
            t = (z + i) % nz
            rc(
                PK.at[c, pl.ds(pl.multiple_of(t * 2 * NJ, 16), 2 * NJ)],
                Q.at[c, pl.ds(pl.multiple_of(z * 2 * NJ, 16), 2 * NJ)],
                s_a.at[c],
                r_a.at[c],
                (to, t * NJ + j),
            ).start()
            return carry

        lax.fori_loop(0, nz, send, 0)

    def blk_of(c, yy, xx, lo, hi):
        return G.at[c, yy * NX + xx, :, pl.ds(lo, hi - lo)]

    def msg(c, n, yy, xx, lo, hi, dev):
        ref = blk_of(c, yy, xx, lo, hi)
        return rc(ref, ref, s_g.at[c, n], r_g.at[c, n], dev)

    def level0(c):
        return (
            msg(c, 0, y, x, 0, d, dev_r),
            msg(c, 1, y, x, 0, d, dev_l),
            msg(c, 2, y, x, 0, d, dev_y),
        )

    def level1(c):
        return (
            msg(c, 3, y, xl, 0, ca, dev_r),
            msg(c, 4, y, xr, ca, d, dev_l),
            msg(c, 5, y, xl, ca, d, dev_y),
            msg(c, 6, y, xr, ca, d, dev_y),
            msg(c, 7, yo, x, 0, ca, dev_r),
            msg(c, 8, yo, x, 0, ca, dev_l),
        )

    def level2(c):
        return (
            msg(c, 9, y, x2, ca, d, dev_y),
            msg(c, 10, yo, xl, 0, qa, dev_r),
            msg(c, 11, yo, xr, qa, ca, dev_l),
        )

    def stage_b(c):
        drain(Q.at[c], r_a.at[c])
        u = jnp.dot(T1[...], Q[c], preferred_element_type=F32)
        sq = jnp.zeros((blk, 1), F32)
        for o in range(NJ):
            v = u[o * blk : (o + 1) * blk]
            sq = sq + jnp.sum(v * v, axis=1, keepdims=True)
        inv = lax.rsqrt(sq / d + 1e-6)
        for o in range(NJ):
            v = u[o * blk : (o + 1) * blk]
            G[c, j, :, o * oc : (o + 1) * oc] = (v * inv * GS[:, o * oc : (o + 1) * oc]).astype(BF16)
        for s in level0(c)[::-1]:
            s.start()

    def stage_l1(c):
        a, b, w = level0(c)
        m3, m4, m5, m6, m7, m8 = level1(c)
        a.wait_recv()
        m3.start()
        m5.start()
        b.wait_recv()
        m4.start()
        m6.start()
        w.wait_recv()
        m7.start()
        m8.start()

    def stage_l2(c):
        _, m4, _, _, m7, m8 = level1(c)
        m9, m10, m11 = level2(c)
        m4.wait_recv()
        m9.start()
        m7.wait_recv()
        m10.start()
        m8.wait_recv()
        m11.start()

    def stage_d(c):
        m3, _, m5, m6, _, _ = level1(c)
        for s in (m3, m5, m6) + level2(c):
            s.wait_recv()
        kb = d // 7 if d % (7 * 128) == 0 else 128

        def step(i, acc):
            cols = pl.ds(pl.multiple_of(i * kb, 128), kb)
            rows = G[c, :, :, cols].reshape(NJ * blk, kb)
            return acc + jnp.dot(rows, W[cols, :], preferred_element_type=F32)

        acc = lax.fori_loop(0, d // kb, step, jnp.zeros((NJ * blk, 2 * nf), F32))
        gate, up = acc[:, 0:nf], acc[:, nf : 2 * nf]
        H[c, x] = (gate / (1.0 + jnp.exp(-gate)) * up).astype(BF16)

        def send(t, dev):
            rc(H.at[c, x], H.at[c, x], s_h.at[c], r_h.at[c], dev).start()

        on_row(send)

    def to_y(c):
        return rc(OY.at[c], YR.at[c], s_y.at[c], r_y.at[c], dev_y)

    def stage_e(c):
        drain(H.at[c, pl.ds(0, NX - 1)], r_h.at[c])

        def down(yy):
            rows = pl.ds(pl.multiple_of(yy * half, half), half)
            hid = jnp.concatenate([H[c, i, rows] for i in range(NX)], axis=1)
            return jnp.dot(hid, WD[...], preferred_element_type=F32)

        OY[c] = down(yo).astype(BF16)
        to_y(c).start()
        PF[c] = down(y)

    def stage_s(c):
        to_y(c).wait_recv()
        SR[c] = (PF[c] + YR[c].astype(F32)).astype(BF16)

        def octant(h):
            return pl.ds(pl.multiple_of((2 * x + h) * blk, blk), blk)

        def rows(t):
            return pl.ds(pl.multiple_of(t * blk, blk), blk)

        for h in range(2):
            B[c, octant(h)] = SR[c, rows(x), h * oc : (h + 1) * oc]

        def send(t, dev):
            for h in range(2):
                rc(
                    SR.at[c, rows(t), pl.ds(h * oc, oc)],
                    B.at[c, octant(h)],
                    s_b.at[c],
                    r_b.at[c],
                    dev,
                ).start()

        on_row(send)

    def stage_f(c):
        drain(B.at[c, pl.ds(0, 2 * (NX - 1) * blk)], r_b.at[c])
        C[c] = jnp.dot(T2[...], B[c], preferred_element_type=F32).astype(BF16)
        own = pl.ds(pl.multiple_of(z * 2 * NJ, 16), 2 * NJ)
        F[c, own] = C[c, own]

        def send(i, carry):
            t = (z + i) % nz
            rc(
                C.at[c, pl.ds(pl.multiple_of(t * 2 * NJ, 16), 2 * NJ)],
                F.at[c, own],
                s_f.at[c],
                r_f.at[c],
                (p, t * NJ + j),
            ).start()
            return carry

        lax.fori_loop(1, nz, send, 0)

    def spread(m):
        rt = RP[m]
        af = AP[m]
        share = route_scale * af / jnp.sum(af, axis=0, keepdims=True)
        weight = jnp.zeros((mr, lanes), F32)
        for k in range(rt.shape[0]):
            weight = weight + jnp.where(rt[k : k + 1, :] == zrow, share[k : k + 1, :], 0.0)
        chosen, rank = slots(rt)
        olane = (iot((tok, mr), 1) // 2) % NJ
        for k in range(2):
            s = jnp.where((chosen > 0.0) & (rank == 2 * k + crow), weight, 0.0)
            s = jnp.transpose(s)[0:tok]
            hi = s.astype(BF16).astype(F32)
            lo = s - hi
            for h, v in ((0, hi), (1, lo)):
                for o in range(NJ):
                    SP[m, h, o * tok : (o + 1) * tok, k * mr : (k + 1) * mr] = jnp.where(
                        olane == o, v, 0.0
                    ).astype(BF16)

    def stage_g(m):
        for k in range(2):
            drain(F.at[2 * m + k, pl.ds(0, (nz - 1) * 2 * NJ)], r_f.at[2 * m + k])
        rows = F[pl.ds(2 * m, 2)].reshape(2 * mr, oc)
        res = jnp.dot(SP[m, 0], rows, preferred_element_type=F32)
        res = res + jnp.dot(SP[m, 1], rows, preferred_element_type=F32)
        for o in range(NJ):
            OUT[m, :, o * oc : (o + 1) * oc] = res[o * tok : (o + 1) * tok].astype(BF16)

    def pack_loop(c, carry):
        stage_a(c)
        send_a(c)
        return carry

    lax.fori_loop(0, NCH, pack_loop, 0)
    r_ = iot((mr, mr), 0)
    c_ = iot((mr, mr), 1)
    hit = (
        (r_ // blk == (c_ // 2) % NJ) & ((r_ // 2) % nz == c_ // (2 * NJ)) & (r_ % 2 == c_ % 2)
    )
    T1[...] = hit.astype(F32).astype(BF16)
    hit2 = (
        (c_ // blk == (r_ // 2) % NJ) & ((c_ // 2) % nz == r_ // (2 * NJ)) & (r_ % 2 == c_ % 2)
    )
    T2[...] = hit2.astype(F32).astype(BF16)

    def gain_block(k, carry):
        s = scales[z, k]
        f = jnp.where(s > 0, 2.0, jnp.where(s < 0, 0.5, 1.0)).astype(F32)
        cols = pl.ds(pl.multiple_of(k * 128, 128), 128)
        GS[:, cols] = gain[:, cols] * f
        return carry

    lax.fori_loop(0, d // 128, gain_block, 0)

    spread(0)
    spread(1)

    def main(it, carry):
        def when(lag, f):
            c = it - lag
            pl.when((c >= 0) & (c < NCH))(lambda: f(c))

        when(0, stage_b)
        when(1, stage_l1)
        when(2, stage_l2)

        @pl.when(it == 3)
        def _():
            local[2].wait()
            local[3].wait()
            local[4].wait()
            drain(WD.at[pl.ds(0, (NX - 1) * nf)], r_wd.at[0])

        when(3, stage_d)
        when(4, stage_e)
        when(5, stage_s)
        when(6, stage_f)

        @pl.when(it == 8)
        def _():
            stage_g(0)
            pltpu.make_async_copy(OUT.at[0], oute, s_out.at[0]).start()

        @pl.when(it == 10)
        def _():
            stage_g(1)
            pltpu.make_async_copy(OUT.at[1], outw, s_out.at[1]).start()

        return carry

    lax.fori_loop(0, 11, main, 0)

    rt_e.wait_send()
    rt_w.wait_send()
    drain(WD.at[pl.ds(0, (NX - 1) * nf)], s_wd.at[0])

    def finish(c, carry):
        for s in level0(c) + level1(c) + level2(c):
            s.wait_send()
        drain(H.at[c, pl.ds(0, NX - 1)], s_h.at[c])
        to_y(c).wait_send()
        drain(B.at[c, pl.ds(0, 2 * (NX - 1) * blk)], s_b.at[c])
        drain(C.at[c, pl.ds(0, (nz - 1) * 2 * NJ)], s_f.at[c])
        return carry

    lax.fori_loop(0, NCH, finish, 0)
    for c in range(NCH):
        drain(PK.at[c], s_a.at[c])
    pltpu.make_async_copy(OUT.at[0], oute, s_out.at[0]).wait()
    pltpu.make_async_copy(OUT.at[1], outw, s_out.at[1]).wait()


def body(mesh_shape, xe, xw, rte, rtw, afe, afw, gain, wg, wu, wd, scales):
    np_, ne = mesh_shape
    nz = ne // NJ
    _, tok, d = xe.shape
    nf = wg.shape[2]
    oc = d // NJ
    mr = nz * NJ * 2
    blk = 2 * nz
    top = rte.shape[2]
    any_, hbm = pl.BlockSpec(memory_space=pl.ANY), pl.BlockSpec(memory_space=pltpu.HBM)
    dma = pltpu.SemaphoreType.DMA
    flops = 2 * NCH * NJ * blk * d * 3 * nf
    moved = 2 * 2 * (4 * tok * d + 3 * d * nf)
    outs = pl.pallas_call(
        functools.partial(kernel, np_, nz, d, tok, nf),
        out_shape=[jax.ShapeDtypeStruct((tok, d), BF16)] * 2,
        in_specs=[hbm] * 10 + [pl.BlockSpec(memory_space=pltpu.SMEM)],
        out_specs=[any_, any_],
        scratch_shapes=[
            pltpu.VMEM((2, top, tok), I32),
            pltpu.VMEM((2, top, tok), F32),
            pltpu.VMEM((1, d), F32),
            pltpu.VMEM((2, tok, d), BF16),
            pltpu.VMEM((2, top, 128), I32),
            pltpu.VMEM((2, top, 128), I32),
            pltpu.VMEM((2, top, 128), F32),
            pltpu.VMEM((d, 2 * nf), BF16),
            pltpu.VMEM((NX * nf, d // NX), BF16),
            pltpu.VMEM((1, d), F32),
            pltpu.VMEM((mr, mr), BF16),
            pltpu.VMEM((mr, mr), BF16),
            pltpu.VMEM((NCH, mr, oc), BF16),
            pltpu.VMEM((NCH, mr, oc), BF16),
            pltpu.VMEM((NCH, NJ, blk, d), BF16),
            pltpu.VMEM((NCH, NX, NJ * blk, nf), BF16),
            pltpu.VMEM((NCH, NX * blk, d // NX), BF16),
            pltpu.VMEM((NCH, NX * blk, d // NX), BF16),
            pltpu.VMEM((NCH, NX * blk, d // NX), F32),
            pltpu.VMEM((NCH, NX * blk, d // NX), BF16),
            pltpu.VMEM((NCH, NJ * blk, oc), BF16),
            pltpu.VMEM((NCH, mr, oc), BF16),
            pltpu.VMEM((NCH, mr, oc), BF16),
            pltpu.VMEM((2, 2, NJ * tok, 2 * mr), BF16),
            pltpu.VMEM((2, tok, d), BF16),
            dma((5,)),
            dma((5,)),
            dma((2,)),
            dma((2,)),
            dma((2,)),
            dma((1,)),
            dma((1,)),
            dma((NCH,)),
            dma((NCH,)),
            dma((NCH, 12)),
            dma((NCH, 12)),
            dma((NCH,)),
            dma((NCH,)),
            dma((NCH,)),
            dma((NCH,)),
            dma((NCH,)),
            dma((NCH,)),
            dma((NCH,)),
            dma((NCH,)),
        ],
        compiler_params=pltpu.CompilerParams(
            collective_id=0, has_side_effects=True, vmem_limit_bytes=56 * 2**20
        ),
        cost_estimate=pl.CostEstimate(flops=flops, bytes_accessed=moved, transcendentals=0),
    )(
        xe[0], xw[0], rte[0].T, rtw[0].T, afe[0].T, afw[0].T, gain,
        wg[0], wu[0], wd[0], scales[0],
    )
    return outs[0][None], outs[1][None]


def solution(mesh):
    tokens = P("pipe", "expert", None)
    placed = (tokens,) * 6 + (
        P("pipe", None),
        P("pipe", None, "expert"),
        P("pipe", None, "expert"),
        P("pipe", "expert", None),
        P("pipe", None, None),
    )
    return jax.shard_map(
        functools.partial(body, (mesh.shape["pipe"], mesh.shape["expert"])),
        mesh=mesh,
        in_specs=placed,
        out_specs=(tokens, tokens),
        check_vma=False,
    )
```
